32 devices in a mesh: section: 4 (over x, core), seq: 8 (over z, y).
Axes of the slice: x: 2, y: 2, z: 4, core: 2. Of those that a mesh axis runs over, the one named last changes fastest.
Arguments:
- residual: bfloat16 [4, 2048, 2048], P('section', 'seq'), may hold values from -6 to 6
- w_qkv: bfloat16 [4, 2048, 6144], P('section', 'seq'), may hold values from -0.125 to 0.125
- w_beta: bfloat16 [4, 2048, 16], P('section', 'seq'), may hold values from -0.125 to 0.125
- beta_bias: float32 [4, 16], P('section'), may hold values from -8 to 2
- norm_gain: float32 [4, 2048], P('section'), may hold values from 0.1 to 1.9
- out_gain: float32 [4, 128], P('section'), may hold values from 0.1 to 1.9
- state_in: float32 [4, 16, 128, 128], P('section'), may hold values from -6 to 6
- doc_start: int32 [2, 4], P(None, 'section'), may hold values from 0 to 32, as said below
Outputs:
- stream_out: bfloat16 [4, 2048, 2048], P('section', 'seq')
The draws below stay inside these ranges and needn't reach their ends.
Inputs may be any that keep to these rules, and one draw needn't show every extreme that they name: `doc_start`: 32 means no new document in that micro-batch.
All inputs are finite; a program needn't handle non-finite values.
Results may differ from the reference program's by a relative error of at most 0.03.
Values may be sent and summed in bfloat16 or wider, within the bound.
A program may use at most 192 MiB of HBM per device.

```python
import jax
import jax.numpy as jnp
from jax import lax

HEADS = 16
HD = 128
D = 2048
GROUP = 64
TICKS = 2
LAYERS = 4
SEQ = 2048
NCH = 32


def draw_beta_bias(key, part):
    return jax.random.uniform(key, (LAYERS, HEADS), jnp.float32, -7.0, 2.0)


def draw_doc_start(key, part):
    drawn = jax.random.randint(key, (TICKS, LAYERS), 0, NCH + 1, dtype=jnp.int32)
    drawn = drawn.at[0, 0].set(NCH)
    return drawn.at[1, 0].set(0)


def levels(rng, extent, split, low, high):
    level, own = 1.0, jax.random.fold_in(rng, 6)
    for dim, blocks in split:
        draws = jnp.exp(jax.random.uniform(jax.random.fold_in(own, dim), (blocks,), jnp.float32, low / len(split), high / len(split)))
        level = level * jnp.repeat(draws, extent[dim] // blocks).reshape([-1 if axis == dim else 1 for axis in range(len(extent))])
    return level


def scatter_about(rng, extent, deviation, most, cuts=(), kind=jnp.bfloat16):
    entries = deviation * jax.random.normal(rng, extent, jnp.float32)
    if cuts:
        entries = entries * levels(rng, extent, cuts, -0.22, 0.18)
    return jnp.clip(entries, -most, most).astype(kind)


def setup_inputs(seed: int = 0) -> dict:
    key_of = jax.random.split(jax.random.key(seed), 9)
    return {
        "residual": scatter_about(key_of[0], (LAYERS, SEQ, D), 1.0, 6.0, ((0, 4), (1, 8))),
        "w_qkv": scatter_about(key_of[1], (LAYERS, D, 3 * D), D ** -0.5, 0.125, ((0, 4), (1, 8))),
        "w_beta": scatter_about(key_of[2], (LAYERS, D, HEADS), D ** -0.5, 0.125, ((0, 4), (1, 8))),
        "beta_bias": draw_beta_bias(jax.random.fold_in(key_of[8], 71), 0),
        "norm_gain": jnp.clip(1.0 + 0.18 * jax.random.normal(key_of[4], (LAYERS, D), jnp.float32), 0.1, 1.9),
        "out_gain": jnp.clip(1.0 + 0.18 * jax.random.normal(key_of[5], (LAYERS, HD), jnp.float32), 0.1, 1.9),
        "state_in": scatter_about(key_of[6], (LAYERS, HEADS, HD, HD), 1.0, 6.0, ((0, 4),), jnp.float32),
        "doc_start": draw_doc_start(jax.random.fold_in(key_of[8], 71), 0),
    }


FULL_PRECISION = lax.Precision.HIGHEST

def unit_norm(projected):
    return projected * lax.rsqrt(lax.optimization_barrier(jnp.sum(projected * projected, axis=-1, keepdims=True)) + 1e-06)

def block_solve(key_rows, values, beta_rows):
    block_len = key_rows.shape[-2]
    intersections = jnp.einsum('ghik,ghjk->ghij', key_rows, key_rows, precision=FULL_PRECISION)
    system = jnp.tril(intersections * beta_rows[..., :, None], -1) + jnp.eye(block_len, dtype=jnp.float32)
    right_side = jnp.concatenate([values * beta_rows[..., None], key_rows * beta_rows[..., None]], axis=-1)
    solved = lax.linalg.triangular_solve(system, right_side, left_side=True, lower=True, unit_diagonal=True)
    head_width = values.shape[-1]
    return (solved[..., :head_width], solved[..., head_width:])

def prepare(stream, weight_qkv, weight_beta, head_bias, in_gain):
    row_count = stream.shape[0]
    widened = stream.astype(jnp.float32)
    normed = (widened * lax.rsqrt(lax.optimization_barrier(jnp.mean(widened * widened, axis=-1, keepdims=True)) + 1e-05) * in_gain).astype(jnp.bfloat16)
    projected = jnp.dot(normed.astype(jnp.float32), weight_qkv.astype(jnp.float32), preferred_element_type=jnp.float32).reshape(row_count, 3, HEADS, HD)
    queries = unit_norm(projected[:, 0]).astype(jnp.bfloat16)
    key_rows = unit_norm(projected[:, 1]).astype(jnp.bfloat16)
    values = projected[:, 2].astype(jnp.bfloat16)
    beta_rows = jax.nn.sigmoid(jnp.dot(normed.astype(jnp.float32), weight_beta.astype(jnp.float32), preferred_element_type=jnp.float32) + head_bias)
    blocks = row_count // GROUP

    def to_blocks(tensor):
        return tensor.astype(jnp.float32).reshape(blocks, GROUP, HEADS, HD).transpose(0, 2, 1, 3)
    beta_blk = beta_rows.reshape(blocks, GROUP, HEADS).transpose(0, 2, 1)
    key_block = to_blocks(key_rows)
    inject, weights = block_solve(key_block, to_blocks(values), beta_blk)
    return (to_blocks(queries), key_block, inject, weights, widened)

def run_blocks(queries, key_rows, inject, weights, current_state, doc_block, first_block):
    block_count = queries.shape[0]
    block_len = queries.shape[2]
    causal = jnp.tril(jnp.ones((block_len, block_len), jnp.float32))

    def advance(current_state, pieces):
        query_block, key_block, inject_block, weight_block, block_index = pieces
        current_state = jnp.where(block_index == doc_block, jnp.zeros_like(current_state), current_state)
        delta_values = inject_block - jnp.einsum('jxy,jyu->jxu', weight_block, current_state, precision=FULL_PRECISION)
        attention_scores = jnp.einsum('hik,hjk->hij', query_block, key_block, precision=FULL_PRECISION) * causal
        block_result = jnp.einsum('jxy,jyu->jxu', query_block, current_state, precision=FULL_PRECISION) + jnp.einsum('ucd,udo->uco', attention_scores, delta_values, precision=FULL_PRECISION)
        current_state = current_state + jnp.einsum('plq,plw->pqw', key_block, delta_values, precision=FULL_PRECISION)
        return (current_state, block_result)
    block_ids = first_block + jnp.arange(block_count, dtype=jnp.int32)
    return lax.scan(advance, current_state, (queries, key_rows, inject, weights, block_ids))

def finish(widened, block_result, head_gain):
    blocks = block_result.shape[0]
    mixed = block_result.transpose(0, 2, 1, 3).reshape(blocks * GROUP, HEADS, HD)
    mixed = mixed * lax.rsqrt(lax.optimization_barrier(jnp.mean(mixed * mixed, axis=-1, keepdims=True)) + 1e-05) * head_gain
    return (widened + mixed.reshape(blocks * GROUP, HEADS * HD)).astype(jnp.bfloat16)

def reference(residual, w_qkv, w_beta, beta_bias, norm_gain, out_gain, state_in, doc_start):

    def segment_pass(pieces):
        stream, weight_qkv, weight_beta, head_bias, in_gain, head_gain, given_state, doc_block = pieces
        queries, key_rows, inject, weights, widened = prepare(stream, weight_qkv, weight_beta, head_bias, in_gain)
        final_state, block_result = run_blocks(queries, key_rows, inject, weights, given_state, doc_block, jnp.int32(0))
        return (finish(widened, block_result, head_gain), final_state)
    stream = residual
    carried = state_in
    outputs = residual
    for tick_index in range(TICKS):
        outputs, carried = lax.map(segment_pass, (stream, w_qkv, w_beta, beta_bias, norm_gain, out_gain, carried, doc_start[tick_index]))
        stream = jnp.roll(outputs, 1, axis=0)
    return outputs
```

```python
import functools

import jax
import jax.numpy as jnp
from jax import lax
from jax.experimental import pallas as pl
from jax.experimental.pallas import tpu as pltpu
from jax.sharding import PartitionSpec as P

HEADS = 16
HD = 128
GROUP = 64
TICKS = 2
CHUNK = 128
F32 = jnp.float32
BF16 = jnp.bfloat16


def mm(a, b):
    return jnp.dot(a.astype(BF16), b.astype(BF16), preferred_element_type=F32)


def mm_nt(a, b):
    return lax.dot_general(
        a.astype(BF16), b.astype(BF16), (((1,), (1,)), ((), ())), preferred_element_type=F32
    )


def unit_norm(p):
    return p * lax.rsqrt(jnp.sum(p * p, axis=-1, keepdims=True) + 1e-06)


def layer_rows(normed, w, bias, out_gain, residual, state, heads, doc_block, first_block):
    rows = normed.shape[0]
    width = heads * HD
    projected = jnp.dot(normed, w, preferred_element_type=F32)
    row = lax.broadcasted_iota(jnp.int32, (CHUNK, CHUNK), 0)
    col = lax.broadcasted_iota(jnp.int32, (CHUNK, CHUNK), 1)
    row1 = lax.broadcasted_iota(jnp.int32, (CHUNK, 1), 0)
    eye = (row == col).astype(F32)
    problems = []
    for h in range(heads):
        q_all = unit_norm(projected[:, h * HD : (h + 1) * HD]).astype(BF16)
        k_all = unit_norm(projected[:, width + h * HD : width + (h + 1) * HD])
        k_all = k_all.astype(BF16).astype(F32)
        v_all = projected[:, 2 * width + h * HD : 2 * width + (h + 1) * HD]
        beta_all = jax.nn.sigmoid(
            projected[:, 3 * width + h : 3 * width + h + 1] + bias[:, h : h + 1]
        )
        for c in range(rows // CHUNK):
            at = slice(c * CHUNK, (c + 1) * CHUNK)
            problems.append((h, c, q_all[at], k_all[at], v_all[at], beta_all[at]))
    systems, inverses, masks = [], [], []
    for h, c, q, k, v, beta in problems:
        start = (doc_block - first_block) * GROUP - c * CHUNK
        inside = jnp.logical_and(start >= 0, start < CHUNK)
        cut = jnp.where(inside, start, 0)
        late_row = row >= cut
        late_col = col >= cut
        same = late_row == late_col
        from_entry = jnp.where(inside, (row1 < cut).astype(F32), 1.0)
        to_exit = (row1 >= cut).astype(F32)
        keep = jnp.where(inside, 0.0, 1.0)
        system = jnp.where(jnp.logical_and(row > col, same), mm_nt(k * beta, k), 0.0)
        systems.append(system)
        masks.append((same, from_entry, to_exit, keep))
        inverses.append(eye - jnp.where((row // 2) == (col // 2), system, 0.0))
    size = 2
    while size < CHUNK:
        level = jnp.logical_and(
            (row // (2 * size)) == (col // (2 * size)), (row // size) != (col // size)
        )
        halves = [mm(jnp.where(level, s, 0.0), x) for s, x in zip(systems, inverses)]
        inverses = [x - mm(x, b) for x, b in zip(inverses, halves)]
        size *= 2
    steps = {}
    for (h, c, q, k, v, beta), inverse, (same, from_entry, to_exit, keep) in zip(
        problems, inverses, masks
    ):
        solved = mm(inverse, jnp.concatenate([v * beta, k * (beta * from_entry)], axis=1))
        scores = jnp.where(jnp.logical_and(row >= col, same), mm_nt(q, k), 0.0)
        lhs = jnp.concatenate([scores, jnp.transpose(k * to_exit)], axis=0)
        both = mm(lhs, solved)
        add = both[:, :HD]
        q_in = q.astype(F32) * from_entry
        through = jnp.concatenate([q_in - both[:CHUNK, HD:], -both[CHUNK:, HD:]], axis=0)
        steps[h, c] = (through.astype(BF16), add, keep)
    pieces = []
    for c in range(rows // CHUNK):
        for h in range(heads):
            through, add, keep = steps[h, c]
            now = state[h]
            moved = jnp.dot(through, now.astype(BF16), preferred_element_type=F32) + add
            state[h] = now * keep + moved[CHUNK:]
            pieces.append(moved[:CHUNK])
    columns = []
    for h in range(heads):
        o = jnp.concatenate([pieces[c * heads + h] for c in range(rows // CHUNK)], axis=0)
        columns.append(
            o * lax.rsqrt(jnp.mean(o * o, axis=-1, keepdims=True) + 1e-05) * out_gain
        )
    mixed = jnp.concatenate(columns, axis=1) if heads > 1 else columns[0]
    return (residual.astype(F32) + mixed).astype(BF16)


def layer_kernel(heads, parts, info, x, w, bias, in_gain, out_gain, entry, out, final):
    step = pl.program_id(0)
    width = heads * HD

    @pl.when(step == 0)
    def _():
        final[...] = entry[...]

    if parts:
        wide = jnp.concatenate([x[c] for c in range(parts)], axis=1).astype(F32)
        residual = x[info[1]]
    else:
        wide = x[...].astype(F32)
        residual = x[:, pl.ds(pl.multiple_of(info[1] * width, HD), width)]
    normed = wide * lax.rsqrt(jnp.mean(wide * wide, axis=-1, keepdims=True) + 1e-05) * in_gain[...]
    rows = wide.shape[0]
    state = [final[h] for h in range(heads)]
    out[...] = layer_rows(
        normed.astype(BF16), w[...], bias[...], out_gain[...], residual, state, heads,
        info[0], step * (rows // GROUP),
    )
    for h in range(heads):
        final[h] = state[h]


def layer(x, w, bias, in_gain, out_gain, entry, info, heads, rows=512):
    parts = x.shape[0] if x.ndim == 3 else 0
    total, d = x.shape[-2], in_gain.shape[-1]
    width = heads * HD
    if parts:
        x_spec = pl.BlockSpec((parts, rows, x.shape[2]), lambda i, s: (0, i, 0))
    else:
        x_spec = pl.BlockSpec((rows, d), lambda i, s: (i, 0))

    def whole(shape):
        return pl.BlockSpec(shape, lambda i, s: (0,) * len(shape))

    return pl.pallas_call(
        functools.partial(layer_kernel, heads, parts),
        out_shape=(
            jax.ShapeDtypeStruct((total, width), BF16),
            jax.ShapeDtypeStruct((heads, HD, HD), F32),
        ),
        grid_spec=pltpu.PrefetchScalarGridSpec(
            num_scalar_prefetch=1,
            grid=(total // rows,),
            in_specs=[
                x_spec,
                whole(w.shape),
                whole(bias.shape),
                whole(in_gain.shape),
                whole(out_gain.shape),
                whole(entry.shape),
            ],
            out_specs=(
                pl.BlockSpec((rows, width), lambda i, s: (i, 0)),
                whole((heads, HD, HD)),
            ),
        ),
        compiler_params=pltpu.CompilerParams(vmem_limit_bytes=50 * 2**20),
        name="layer",
    )(info, x, w, bias, in_gain, out_gain, entry)


def shards(residual, w_qkv, w_beta, beta_bias, norm_gain, out_gain, state_in, doc_start):
    count = lax.axis_size("seq")
    place = lax.axis_index("seq")
    heads = HEADS // count
    width = heads * HD
    depth = w_qkv.shape[1]
    weights = jnp.concatenate(
        [
            w_qkv[0].reshape(depth, 3, count, width).transpose(2, 0, 1, 3).reshape(count, depth, 3 * width),
            jnp.pad(
                w_beta[0].reshape(depth, count, heads).transpose(1, 0, 2),
                ((0, 0), (0, 0), (0, HD - heads)),
            ),
        ],
        axis=2,
    )
    weights = lax.all_to_all(weights, "seq", 0, 0, tiled=True).reshape(count * depth, 3 * width + HD)
    stream = lax.all_gather(residual[0], "seq", axis=0, tiled=True)
    bias = lax.dynamic_slice(beta_bias, (0, place * heads), (1, heads))
    bias = jnp.pad(bias, ((0, 0), (0, HD - heads)))
    state = lax.dynamic_slice(state_in[0], (place * heads, 0, 0), (heads, HD, HD))
    out = None
    for tick in range(TICKS):
        if tick:
            out = lax.ppermute(
                out, "section", [(i, (i + 1) % lax.axis_size("section")) for i in range(lax.axis_size("section"))]
            )
            stream = lax.all_gather(out, "seq", axis=0)
        info = jnp.stack([doc_start[tick, 0], place]).astype(jnp.int32)
        out, state = layer(stream, weights, bias, norm_gain, out_gain, state, info, heads)
    back = lax.all_to_all(out.reshape(count, -1, width), "seq", 0, 0, tiled=True)
    return back.transpose(1, 0, 2).reshape(1, -1, count * width)


def solution(mesh):
    return jax.shard_map(
        shards,
        mesh=mesh,
        in_specs=(
            P("section", "seq", None),
            P("section", "seq", None),
            P("section", "seq", None),
            P("section", None),
            P("section", None),
            P("section", None),
            P("section", None, None, None),
            P(None, "section"),
        ),
        out_specs=P("section", "seq", None),
        check_vma=False,
    )
```

```python
import functools

import jax
import jax.numpy as jnp
from jax import lax
from jax.experimental import pallas as pl
from jax.experimental.pallas import tpu as pltpu
from jax.sharding import PartitionSpec as P

HEADS = 16
HD = 128
GROUP = 64
TICKS = 2
CHUNK = 128
F32 = jnp.float32
BF16 = jnp.bfloat16


def mm(a, b):
    return jnp.dot(a.astype(BF16), b.astype(BF16), preferred_element_type=F32)


def mm_nt(a, b):
    return lax.dot_general(
        a.astype(BF16), b.astype(BF16), (((1,), (1,)), ((), ())), preferred_element_type=F32
    )


def unit_norm(p):
    return p * lax.rsqrt(jnp.sum(p * p, axis=-1, keepdims=True) + 1e-06)


def layer_rows(
    normed, w, wb, bias, out_gain, residual, state, heads, first_head, doc_block, first_block
):
    rows = normed.shape[0]
    width = heads * HD
    projected = jnp.dot(normed, w, preferred_element_type=F32)
    logits = mm_nt(normed, wb) + bias
    row = lax.broadcasted_iota(jnp.int32, (CHUNK, CHUNK), 0)
    col = lax.broadcasted_iota(jnp.int32, (CHUNK, CHUNK), 1)
    row1 = lax.broadcasted_iota(jnp.int32, (CHUNK, 1), 0)
    eye = (row == col).astype(F32)
    problems = []
    for h in range(heads):
        q_all = unit_norm(projected[:, h * HD : (h + 1) * HD]).astype(BF16)
        k_all = unit_norm(projected[:, width + h * HD : width + (h + 1) * HD])
        k_all = k_all.astype(BF16).astype(F32)
        v_all = projected[:, 2 * width + h * HD : 2 * width + (h + 1) * HD]
        mine = lax.broadcasted_iota(jnp.int32, logits.shape, 1) == first_head + h
        beta_all = jax.nn.sigmoid(
            jnp.sum(jnp.where(mine, logits, 0.0), axis=-1, keepdims=True)
        )
        for c in range(rows // CHUNK):
            at = slice(c * CHUNK, (c + 1) * CHUNK)
            problems.append((h, c, q_all[at], k_all[at], v_all[at], beta_all[at]))
    systems, inverses, masks = [], [], []
    for h, c, q, k, v, beta in problems:
        start = (doc_block - first_block) * GROUP - c * CHUNK
        inside = jnp.logical_and(start >= 0, start < CHUNK)
        cut = jnp.where(inside, start, 0)
        late_row = row >= cut
        late_col = col >= cut
        same = late_row == late_col
        from_entry = jnp.where(inside, (row1 < cut).astype(F32), 1.0)
        to_exit = (row1 >= cut).astype(F32)
        keep = jnp.where(inside, 0.0, 1.0)
        system = jnp.where(jnp.logical_and(row > col, same), mm_nt(k * beta, k), 0.0)
        systems.append(system)
        masks.append((same, from_entry, to_exit, keep))
        inverses.append(eye - jnp.where((row // 2) == (col // 2), system, 0.0))
    size = 2
    while size < CHUNK:
        level = jnp.logical_and(
            (row // (2 * size)) == (col // (2 * size)), (row // size) != (col // size)
        )
        halves = [mm(jnp.where(level, s, 0.0), x) for s, x in zip(systems, inverses)]
        inverses = [x - mm(x, b) for x, b in zip(inverses, halves)]
        size *= 2
    steps = {}
    for (h, c, q, k, v, beta), inverse, (same, from_entry, to_exit, keep) in zip(
        problems, inverses, masks
    ):
        solved = mm(inverse, jnp.concatenate([v * beta, k * (beta * from_entry)], axis=1))
        scores = jnp.where(jnp.logical_and(row >= col, same), mm_nt(q, k), 0.0)
        lhs = jnp.concatenate([scores, jnp.transpose(k * to_exit)], axis=0)
        both = mm(lhs, solved)
        add = both[:, :HD]
        q_in = q.astype(F32) * from_entry
        through = jnp.concatenate([q_in - both[:CHUNK, HD:], -both[CHUNK:, HD:]], axis=0)
        steps[h, c] = (through.astype(BF16), add, keep)
    pieces = []
    for c in range(rows // CHUNK):
        for h in range(heads):
            through, add, keep = steps[h, c]
            now = state[h]
            moved = jnp.dot(through, now.astype(BF16), preferred_element_type=F32) + add
            state[h] = now * keep + moved[CHUNK:]
            pieces.append(moved[:CHUNK])
    columns = []
    for h in range(heads):
        o = jnp.concatenate([pieces[c * heads + h] for c in range(rows // CHUNK)], axis=0)
        columns.append(
            o * lax.rsqrt(jnp.mean(o * o, axis=-1, keepdims=True) + 1e-05) * out_gain
        )
    mixed = jnp.concatenate(columns, axis=1) if heads > 1 else columns[0]
    return (residual.astype(F32) + mixed).astype(BF16)


def layer_kernel(heads, parts, info, x, w, wb, bias, in_gain, out_gain, entry, out, final):
    step = pl.program_id(0)
    width = heads * HD

    @pl.when(step == 0)
    def _():
        final[...] = entry[...]

    if parts:
        wide = jnp.concatenate([x[c] for c in range(parts)], axis=1).astype(F32)
        residual = x[info[1]]
    else:
        wide = x[...].astype(F32)
        residual = x[:, pl.ds(pl.multiple_of(info[1] * width, HD), width)]
    normed = wide * lax.rsqrt(jnp.mean(wide * wide, axis=-1, keepdims=True) + 1e-05) * in_gain[...]
    rows = wide.shape[0]
    state = [final[h] for h in range(heads)]
    out[...] = layer_rows(
        normed.astype(BF16), w[...],
        jnp.concatenate([wb[c] for c in range(wb.shape[0])], axis=1),
        bias[...], out_gain[...], residual, state, heads, info[1] * heads, info[0], step * (rows // GROUP),
    )
    for h in range(heads):
        final[h] = state[h]


def layer(x, w, wb, bias, in_gain, out_gain, entry, info, heads, rows=512):
    parts = x.shape[0] if x.ndim == 3 else 0
    total, d = x.shape[-2], in_gain.shape[-1]
    width = heads * HD
    if parts:
        x_spec = pl.BlockSpec((parts, rows, x.shape[2]), lambda i, s: (0, i, 0))
    else:
        x_spec = pl.BlockSpec((rows, d), lambda i, s: (i, 0))

    def whole(shape):
        return pl.BlockSpec(shape, lambda i, s: (0,) * len(shape))

    return pl.pallas_call(
        functools.partial(layer_kernel, heads, parts),
        out_shape=(
            jax.ShapeDtypeStruct((total, width), BF16),
            jax.ShapeDtypeStruct((heads, HD, HD), F32),
        ),
        grid_spec=pltpu.PrefetchScalarGridSpec(
            num_scalar_prefetch=1,
            grid=(total // rows,),
            in_specs=[
                x_spec,
                whole(w.shape),
                whole(wb.shape),
                whole(bias.shape),
                whole(in_gain.shape),
                whole(out_gain.shape),
                whole(entry.shape),
            ],
            out_specs=(
                pl.BlockSpec((rows, width), lambda i, s: (i, 0)),
                whole((heads, HD, HD)),
            ),
        ),
        compiler_params=pltpu.CompilerParams(vmem_limit_bytes=50 * 2**20),
        name="layer",
    )(info, x, w, wb, bias, in_gain, out_gain, entry)


MESH = pl.DeviceIdType.MESH
Z_CHIPS = 4


def remote(src, dst, send, recv, **to):
    return pltpu.make_async_remote_copy(
        src_ref=src, dst_ref=dst, send_sem=send, recv_sem=recv, device_id=to, device_id_type=MESH
    )


def grid_place():
    count = lax.axis_size("seq")
    nz = min(Z_CHIPS, count)
    ny = count // nz
    place = lax.axis_index("seq")
    return count, nz, ny, place, place // ny, lax.rem(place, ny)


class Spread:
    def __init__(self, slot, blocks, send, recv):
        self.slot, self.blocks, self.send, self.recv = slot, blocks, send, recv
        self.count, self.nz, self.ny, self.place, self.z, self.y = grid_place()
        self.ways = [
            (self.z + 1 < self.nz, self.place + self.ny),
            (self.z > 0, self.place - self.ny),
            (self.y + 1 < self.ny, self.place + 1),
            (self.y > 0, self.place - 1),
        ]

    def neighbours(self):
        return self.ways[: 4 if self.ny > 1 else 2]

    def copy(self, way, source, block, ref=None):
        here = self.slot(source, block)
        return remote(
            here if ref is None else ref,
            here,
            self.send.at[way, source, block],
            self.recv.at[source, block],
            seq=self.ways[way][1],
        )

    def go(self, way, source, block, ref=None):
        if way >= 2 and self.ny == 1:
            return

        @pl.when(self.ways[way][0])
        def _():
            self.copy(way, source, block, ref).start()

    def begin(self, block, ref=None):
        for way in (0, 1, 2, 3):
            self.go(way, self.place, block, ref)

    def arrived(self, source, block):
        self.copy(0, source, block).wait_recv()

    def along_z(self, hop, block):
        for way, sign in ((0, -1), (1, 1)):
            z = self.z + sign * hop

            @pl.when(jnp.logical_and(z >= 0, z < self.nz))
            def _():
                source = z * self.ny + self.y
                self.arrived(source, block)
                if hop + 1 < self.nz:
                    self.go(way, source, block)
                self.go(2, source, block)
                self.go(3, source, block)

    def along_y(self):
        for hop in range(1, self.ny):
            for way, sign in ((2, -1), (3, 1)):
                y = self.y + sign * hop

                @pl.when(jnp.logical_and(y >= 0, y < self.ny))
                def _():
                    def one(i, carry):
                        source, block = (i // self.blocks) * self.ny + y, lax.rem(i, self.blocks)
                        self.arrived(source, block)
                        if hop + 1 < self.ny:
                            self.go(way, source, block)
                        return carry

                    lax.fori_loop(0, self.nz * self.blocks, one, 0)

    def sent(self):
        def one(i, carry):
            source, block = i // self.blocks, lax.rem(i, self.blocks)
            z, y = source // self.ny, lax.rem(source, self.ny)
            lines = [
                jnp.logical_and(y == self.y, z <= self.z),
                jnp.logical_and(y == self.y, z >= self.z),
                y <= self.y,
                y >= self.y,
            ]
            for way in range(4 if self.ny > 1 else 2):

                @pl.when(jnp.logical_and(lines[way], self.ways[way][0]))
                def _():
                    self.copy(way, source, block).wait_send()

            return carry

        lax.fori_loop(0, self.count * self.blocks, one, 0)


def others(count, place):
    return [lax.rem(place + hop, count) for hop in range(1, count)]


def greet_all(count, place):
    barrier = pltpu.get_barrier_semaphore()
    for peer in others(count, place):
        pl.semaphore_signal(barrier, inc=1, device_id={"seq": peer}, device_id_type=MESH)
    pl.semaphore_wait(barrier, count - 1)


def start_kernel(
    x, w, wb, stream, weights, betas, send, recv, w_send, w_recv, b_send, b_recv, own
):
    count, nz, ny, place, _, _ = grid_place()
    depth = w.shape[0]
    width = weights.shape[1] // 3
    greet_all(count, place)
    spread = Spread(lambda source, block: stream.at[source], 1, send, recv)
    spread.begin(0, x)

    def columns(peer, part):
        at = pl.multiple_of((part * count + peer) * width, 128)
        return w.at[:, pl.ds(at, width)]

    def landing(source, part):
        return weights.at[
            pl.ds(pl.multiple_of(source * depth, 16), depth), part * width : (part + 1) * width
        ]

    def beta_copy(hop, peer, source):
        return remote(wb, betas.at[source], b_send.at[hop], b_recv.at[hop], seq=peer)

    def weight_copy(hop, peer, source, part):
        return remote(
            columns(peer, part), landing(source, part), w_send.at[hop, part],
            w_recv.at[hop, part], seq=peer,
        )

    for hop, peer in enumerate(others(count, place)):
        beta_copy(hop, peer, place).start()
        for part in range(3):
            weight_copy(hop, peer, place, part).start()
    local = [
        pltpu.make_async_copy(x, stream.at[place], own.at[0]),
        pltpu.make_async_copy(wb, betas.at[place], own.at[1]),
    ] + [
        pltpu.make_async_copy(columns(place, part), landing(place, part), own.at[2 + part])
        for part in range(3)
    ]
    for one in local:
        one.start()
    for hop in range(1, nz):
        spread.along_z(hop, 0)
    spread.along_y()
    for hop, peer in enumerate(others(count, place)):
        source = lax.rem(place + count - hop - 1, count)
        beta_copy(hop, peer, source).wait_recv()
        beta_copy(hop, peer, place).wait_send()
        for part in range(3):
            weight_copy(hop, peer, source, part).wait_recv()
            weight_copy(hop, peer, place, part).wait_send()
    spread.sent()
    for one in local:
        one.wait()


def start_exchange(x, w, wb):
    count = lax.axis_size("seq")
    any_space = pl.BlockSpec(memory_space=pl.ANY)
    dma = pltpu.SemaphoreType.DMA
    return pl.pallas_call(
        start_kernel,
        out_shape=(
            jax.ShapeDtypeStruct((count,) + x.shape, x.dtype),
            jax.ShapeDtypeStruct((count * w.shape[0], w.shape[1] // count), w.dtype),
            jax.ShapeDtypeStruct((count,) + wb.shape, wb.dtype),
        ),
        in_specs=[any_space] * 3,
        out_specs=(any_space,) * 3,
        scratch_shapes=[
            dma((4, count, 1)),
            dma((count, 1)),
            dma((count - 1, 3)),
            dma((count - 1, 3)),
            dma((count - 1,)),
            dma((count - 1,)),
            dma((5,)),
        ],
        compiler_params=pltpu.CompilerParams(collective_id=0, has_side_effects=True),
        name="start_exchange",
    )(x, w, wb)


def relay_kernel(blocks, out, stream, x_send, x_recv, send, recv):
    count, nz, ny, place, _, _ = grid_place()
    sections = lax.axis_size("section")
    section = lax.axis_index("section")
    after, before = lax.rem(section + 1, sections), lax.rem(section + sections - 1, sections)
    rows = out.shape[0] // blocks

    def slot(source, block):
        at = block * rows
        return stream.at[source, pl.ds(pl.multiple_of(at, 16), rows)]

    spread = Spread(slot, blocks, send, recv)
    barrier = pltpu.get_barrier_semaphore()
    total = 2
    for way, (there, peer) in enumerate(spread.neighbours()):
        total = total + there.astype(jnp.int32)

        @pl.when(there)
        def _():
            pl.semaphore_signal(barrier, inc=1, device_id={"seq": peer}, device_id_type=MESH)

    for peer in (after, before):
        pl.semaphore_signal(barrier, inc=1, device_id={"section": peer}, device_id_type=MESH)
    pl.semaphore_wait(barrier, total)

    def hand_on(block):
        return remote(
            out.at[block * rows : (block + 1) * rows], slot(place, block),
            x_send.at[block], x_recv.at[block], section=after,
        )

    for block in range(blocks):
        hand_on(block).start()
    for step in range(blocks + nz - 1):
        for block in range(blocks):
            hop = step - block
            if hop == 0:
                hand_on(block).wait_recv()
                spread.begin(block)
            elif 0 < hop < nz:
                spread.along_z(hop, block)
    spread.along_y()
    for block in range(blocks):
        hand_on(block).wait_send()
    spread.sent()


def relay(out, blocks=4):
    count = lax.axis_size("seq")
    any_space = pl.BlockSpec(memory_space=pl.ANY)
    dma = pltpu.SemaphoreType.DMA
    return pl.pallas_call(
        functools.partial(relay_kernel, blocks),
        out_shape=jax.ShapeDtypeStruct((count,) + out.shape, out.dtype),
        in_specs=[any_space],
        out_specs=any_space,
        scratch_shapes=[
            dma((blocks,)), dma((blocks,)), dma((4, count, blocks)), dma((count, blocks)),
        ],
        compiler_params=pltpu.CompilerParams(collective_id=1, has_side_effects=True),
        name="relay",
    )(out)


def rows_back_kernel(out, result, send, recv, own):
    count, _, _, place, _, _ = grid_place()
    rows, width = result.shape[0], out.shape[1]
    greet_all(count, place)

    def part(peer):
        return out.at[pl.ds(pl.multiple_of(peer * rows, 16), rows)]

    def columns(source):
        return result.at[:, pl.ds(pl.multiple_of(source * width, 128), width)]

    def copy(hop, peer, source):
        return remote(part(peer), columns(source), send.at[hop], recv.at[hop], seq=peer)

    peers = others(count, place)
    for hop, peer in enumerate(peers):
        copy(hop, peer, place).start()
    mine = pltpu.make_async_copy(part(place), columns(place), own)
    mine.start()
    for hop, peer in enumerate(peers):
        copy(hop, peer, lax.rem(place + count - hop - 1, count)).wait_recv()
        copy(hop, peer, place).wait_send()
    mine.wait()


def rows_back(out):
    count = lax.axis_size("seq")
    any_space = pl.BlockSpec(memory_space=pl.ANY)
    dma = pltpu.SemaphoreType.DMA
    return pl.pallas_call(
        rows_back_kernel,
        out_shape=jax.ShapeDtypeStruct((out.shape[0] // count, out.shape[1] * count), out.dtype),
        in_specs=[any_space],
        out_specs=any_space,
        scratch_shapes=[dma((count - 1,)), dma((count - 1,)), dma(())],
        compiler_params=pltpu.CompilerParams(collective_id=2, has_side_effects=True),
        name="rows_back",
    )(out)


def shards(residual, w_qkv, w_beta, beta_bias, norm_gain, out_gain, state_in, doc_start):
    count = lax.axis_size("seq")
    place = lax.axis_index("seq")
    heads = HEADS // count
    stream, weights, betas = start_exchange(residual[0], w_qkv[0], w_beta[0].T)
    stream = stream.reshape(-1, stream.shape[2])
    state = lax.dynamic_slice(state_in[0], (place * heads, 0, 0), (heads, HD, HD))
    out = None
    for tick in range(TICKS):
        if tick:
            stream = relay(out)
        info = jnp.stack([doc_start[tick, 0], place]).astype(jnp.int32)
        out, state = layer(
            stream, weights, betas, beta_bias, norm_gain, out_gain, state, info, heads
        )
    return rows_back(out)[None]


def solution(mesh):
    return jax.shard_map(
        shards,
        mesh=mesh,
        in_specs=(
            P("section", "seq", None),
            P("section", "seq", None),
            P("section", "seq", None),
            P("section", None),
            P("section", None),
            P("section", None),
            P("section", None, None, None),
            P(None, "section"),
        ),
        out_specs=P("section", "seq", None),
        check_vma=False,
    )
```

```python
import functools

import jax
import jax.numpy as jnp
from jax import lax
from jax.experimental import pallas as pl
from jax.experimental.pallas import tpu as pltpu
from jax.sharding import PartitionSpec as P

HEADS = 16
HD = 128
GROUP = 64
TICKS = 2
CHUNK = 128
F32 = jnp.float32
BF16 = jnp.bfloat16


def mm(a, b):
    return jnp.dot(a.astype(BF16), b.astype(BF16), preferred_element_type=F32)


def mm_nt(a, b):
    return lax.dot_general(
        a.astype(BF16), b.astype(BF16), (((1,), (1,)), ((), ())), preferred_element_type=F32
    )


def unit_norm(p):
    return p * lax.rsqrt(jnp.sum(p * p, axis=-1, keepdims=True) + 1e-06)


def layer_rows(
    normed, w, wb, bias, out_gain, residual, state, heads, first_head, doc_block, first_block
):
    rows = normed.shape[0]
    width = heads * HD
    projected = jnp.dot(normed, w, preferred_element_type=F32)
    logits = mm_nt(normed, wb) + bias
    row = lax.broadcasted_iota(jnp.int32, (CHUNK, CHUNK), 0)
    col = lax.broadcasted_iota(jnp.int32, (CHUNK, CHUNK), 1)
    row1 = lax.broadcasted_iota(jnp.int32, (CHUNK, 1), 0)
    eye = (row == col).astype(F32)
    problems = []
    for h in range(heads):
        q_all = unit_norm(projected[:, h * HD : (h + 1) * HD]).astype(BF16)
        k_all = unit_norm(projected[:, width + h * HD : width + (h + 1) * HD])
        k_all = k_all.astype(BF16).astype(F32)
        v_all = projected[:, 2 * width + h * HD : 2 * width + (h + 1) * HD]
        mine = lax.broadcasted_iota(jnp.int32, logits.shape, 1) == first_head + h
        beta_all = jax.nn.sigmoid(
            jnp.sum(jnp.where(mine, logits, 0.0), axis=-1, keepdims=True)
        )
        for c in range(rows // CHUNK):
            at = slice(c * CHUNK, (c + 1) * CHUNK)
            problems.append((h, c, q_all[at], k_all[at], v_all[at], beta_all[at]))
    systems, inverses, masks = [], [], []
    for h, c, q, k, v, beta in problems:
        start = (doc_block - first_block) * GROUP - c * CHUNK
        inside = jnp.logical_and(start >= 0, start < CHUNK)
        cut = jnp.where(inside, start, 0)
        late_row = row >= cut
        late_col = col >= cut
        same = late_row == late_col
        from_entry = jnp.where(inside, (row1 < cut).astype(F32), 1.0)
        to_exit = (row1 >= cut).astype(F32)
        keep = jnp.where(inside, 0.0, 1.0)
        system = jnp.where(jnp.logical_and(row > col, same), mm_nt(k * beta, k), 0.0)
        systems.append(system)
        masks.append((same, from_entry, to_exit, keep))
        inverses.append(eye - jnp.where((row // 2) == (col // 2), system, 0.0))
    size = 2
    while size < CHUNK:
        level = jnp.logical_and(
            (row // (2 * size)) == (col // (2 * size)), (row // size) != (col // size)
        )
        halves = [mm(jnp.where(level, s, 0.0), x) for s, x in zip(systems, inverses)]
        inverses = [x - mm(x, b) for x, b in zip(inverses, halves)]
        size *= 2
    steps = {}
    for (h, c, q, k, v, beta), inverse, (same, from_entry, to_exit, keep) in zip(
        problems, inverses, masks
    ):
        solved = mm(inverse, jnp.concatenate([v * beta, k * (beta * from_entry)], axis=1))
        scores = jnp.where(jnp.logical_and(row >= col, same), mm_nt(q, k), 0.0)
        lhs = jnp.concatenate([scores, jnp.transpose(k * to_exit)], axis=0)
        both = mm(lhs, solved)
        add = both[:, :HD]
        q_in = q.astype(F32) * from_entry
        through = jnp.concatenate([q_in - both[:CHUNK, HD:], -both[CHUNK:, HD:]], axis=0)
        steps[h, c] = (through.astype(BF16), add, keep)
    pieces = []
    for c in range(rows // CHUNK):
        for h in range(heads):
            through, add, keep = steps[h, c]
            now = state[h]
            moved = jnp.dot(through, now.astype(BF16), preferred_element_type=F32) + add
            state[h] = now * keep + moved[CHUNK:]
            pieces.append(moved[:CHUNK])
    columns = []
    for h in range(heads):
        o = jnp.concatenate([pieces[c * heads + h] for c in range(rows // CHUNK)], axis=0)
        columns.append(
            o * lax.rsqrt(jnp.mean(o * o, axis=-1, keepdims=True) + 1e-05) * out_gain
        )
    mixed = jnp.concatenate(columns, axis=1) if heads > 1 else columns[0]
    return (residual.astype(F32) + mixed).astype(BF16)


MESH = pl.DeviceIdType.MESH
Z_CHIPS = 4


def remote(src, dst, send, recv, **to):
    return pltpu.make_async_remote_copy(
        src_ref=src, dst_ref=dst, send_sem=send, recv_sem=recv, device_id=to, device_id_type=MESH
    )


def grid_place():
    count = lax.axis_size("seq")
    nz = min(Z_CHIPS, count)
    ny = count // nz
    place = lax.axis_index("seq")
    return count, nz, ny, place, place // ny, lax.rem(place, ny)


class Spread:
    def __init__(self, slot, blocks, send, recv):
        self.slot, self.blocks, self.send, self.recv = slot, blocks, send, recv
        self.count, self.nz, self.ny, self.place, self.z, self.y = grid_place()
        self.ways = [
            (self.z + 1 < self.nz, self.place + self.ny),
            (self.z > 0, self.place - self.ny),
            (self.y + 1 < self.ny, self.place + 1),
            (self.y > 0, self.place - 1),
        ]

    def neighbours(self):
        return self.ways[: 4 if self.ny > 1 else 2]

    def copy(self, way, source, block, ref=None):
        here = self.slot(source, block)
        return remote(
            here if ref is None else ref,
            here,
            self.send.at[way, source, block],
            self.recv.at[source, block],
            seq=self.ways[way][1],
        )

    def go(self, way, source, block, ref=None):
        if way >= 2 and self.ny == 1:
            return

        @pl.when(self.ways[way][0])
        def _():
            self.copy(way, source, block, ref).start()

    def begin(self, block, ref=None):
        for way in (0, 1, 2, 3):
            self.go(way, self.place, block, ref)

    def arrived(self, source, block):
        self.copy(0, source, block).wait_recv()

    def along_z(self, hop, block):
        for way, sign in ((0, -1), (1, 1)):
            z = self.z + sign * hop

            @pl.when(jnp.logical_and(z >= 0, z < self.nz))
            def _():
                source = z * self.ny + self.y
                self.arrived(source, block)
                if hop + 1 < self.nz:
                    self.go(way, source, block)
                self.go(2, source, block)
                self.go(3, source, block)

    def along_y(self, block):
        for hop in range(1, self.ny):
            for way, sign in ((2, -1), (3, 1)):
                y = self.y + sign * hop

                @pl.when(jnp.logical_and(y >= 0, y < self.ny))
                def _():
                    for z in range(self.nz):
                        self.arrived(z * self.ny + y, block)
                        if hop + 1 < self.ny:
                            self.go(way, z * self.ny + y, block)

    def sent(self):
        def one(i, carry):
            source, block = i // self.blocks, lax.rem(i, self.blocks)
            z, y = source // self.ny, lax.rem(source, self.ny)
            lines = [
                jnp.logical_and(y == self.y, z <= self.z),
                jnp.logical_and(y == self.y, z >= self.z),
                y <= self.y,
                y >= self.y,
            ]
            for way in range(4 if self.ny > 1 else 2):

                @pl.when(jnp.logical_and(lines[way], self.ways[way][0]))
                def _():
                    self.copy(way, source, block).wait_send()

            return carry

        lax.fori_loop(0, self.count * self.blocks, one, 0)


def others(count, place):
    return [lax.rem(place + hop, count) for hop in range(1, count)]


def greet_all(count, place):
    barrier = pltpu.get_barrier_semaphore()
    for peer in others(count, place):
        pl.semaphore_signal(barrier, inc=1, device_id={"seq": peer}, device_id_type=MESH)
    pl.semaphore_wait(barrier, count - 1)


def start_kernel(
    x, w, wb, stream, weights, betas, send, recv, w_send, w_recv, b_send, b_recv, own
):
    count, nz, ny, place, _, _ = grid_place()
    depth = w.shape[0]
    width = weights.shape[1] // 3
    greet_all(count, place)
    spread = Spread(lambda source, block: stream.at[source], 1, send, recv)
    spread.begin(0, x)

    def columns(peer, part):
        at = pl.multiple_of((part * count + peer) * width, 128)
        return w.at[:, pl.ds(at, width)]

    def landing(source, part):
        return weights.at[
            pl.ds(pl.multiple_of(source * depth, 16), depth), part * width : (part + 1) * width
        ]

    def beta_copy(hop, peer, source):
        return remote(wb, betas.at[source], b_send.at[hop], b_recv.at[hop], seq=peer)

    def weight_copy(hop, peer, source, part):
        return remote(
            columns(peer, part), landing(source, part), w_send.at[hop, part],
            w_recv.at[hop, part], seq=peer,
        )

    for hop, peer in enumerate(others(count, place)):
        beta_copy(hop, peer, place).start()
        for part in range(3):
            weight_copy(hop, peer, place, part).start()
    local = [
        pltpu.make_async_copy(x, stream.at[place], own.at[0]),
        pltpu.make_async_copy(wb, betas.at[place], own.at[1]),
    ] + [
        pltpu.make_async_copy(columns(place, part), landing(place, part), own.at[2 + part])
        for part in range(3)
    ]
    for one in local:
        one.start()
    for hop in range(1, nz):
        spread.along_z(hop, 0)
    spread.along_y(0)
    for hop, peer in enumerate(others(count, place)):
        source = lax.rem(place + count - hop - 1, count)
        beta_copy(hop, peer, source).wait_recv()
        beta_copy(hop, peer, place).wait_send()
        for part in range(3):
            weight_copy(hop, peer, source, part).wait_recv()
            weight_copy(hop, peer, place, part).wait_send()
    spread.sent()
    for one in local:
        one.wait()


def start_exchange(x, w, wb):
    count = lax.axis_size("seq")
    any_space = pl.BlockSpec(memory_space=pl.ANY)
    dma = pltpu.SemaphoreType.DMA
    return pl.pallas_call(
        start_kernel,
        out_shape=(
            jax.ShapeDtypeStruct((count,) + x.shape, x.dtype),
            jax.ShapeDtypeStruct((count * w.shape[0], w.shape[1] // count), w.dtype),
            jax.ShapeDtypeStruct((count,) + wb.shape, wb.dtype),
        ),
        in_specs=[any_space] * 3,
        out_specs=(any_space,) * 3,
        scratch_shapes=[
            dma((4, count, 1)),
            dma((count, 1)),
            dma((count - 1, 3)),
            dma((count - 1, 3)),
            dma((count - 1,)),
            dma((count - 1,)),
            dma((5,)),
        ],
        compiler_params=pltpu.CompilerParams(collective_id=0, has_side_effects=True),
        name="start_exchange",
    )(x, w, wb)


def ticks_kernel(
    blocks, doc, x, w, wb, bias, in_gain, out_gain, entry, result,
    stream, outs, state, x_send, x_recv, send, recv, back_send, back_recv, own,
):
    count, nz, ny, place, _, _ = grid_place()
    sections = lax.axis_size("section")
    section = lax.axis_index("section")
    after, before = lax.rem(section + 1, sections), lax.rem(section + sections - 1, sections)
    heads = HEADS // count
    width = heads * HD
    rows = x.shape[0] // blocks
    share = x.shape[0] // count

    def at(block, size):
        return pl.ds(pl.multiple_of(block * size, 16), size)

    def slot(source, block):
        return stream.at[source, at(block, rows)]

    spread = Spread(slot, blocks, send, recv)
    barrier = pltpu.get_barrier_semaphore()
    for peer in others(count, place):
        pl.semaphore_signal(barrier, inc=1, device_id={"seq": peer}, device_id_type=MESH)
    for peer in (after, before):
        pl.semaphore_signal(barrier, inc=1, device_id={"section": peer}, device_id_type=MESH)
    pl.semaphore_wait(barrier, count + 1)

    def hand_on(block):
        return remote(
            outs.at[0, at(block, rows)], slot(place, block),
            x_send.at[block], x_recv.at[block], section=after,
        )

    def columns(source):
        return result.at[:, pl.ds(pl.multiple_of(source * width, 128), width)]

    def back(peer, source):
        return remote(
            outs.at[1, at(peer, share)], columns(source),
            back_send.at[peer], back_recv.at[source], seq=peer,
        )

    def keep_own():
        return pltpu.make_async_copy(outs.at[1, at(place, share)], columns(place), own)

    def compute(tick, block, wide, residual):
        wide = wide.astype(F32)
        scale = lax.rsqrt(jnp.mean(wide * wide, axis=-1, keepdims=True) + 1e-05)
        normed = (wide * scale * in_gain[...]).astype(BF16)
        now = [state[h] for h in range(heads)]
        outs[tick, at(block, rows)] = layer_rows(
            normed, w[...], jnp.concatenate([wb[c] for c in range(count)], axis=1), bias[...],
            out_gain[...], residual, now, heads, place * heads, doc[tick], block * (rows // GROUP),
        )
        for h in range(heads):
            state[h] = now[h]

    state[...] = entry[...]

    def step(u, carry):
        @pl.when(u < blocks)
        def _():
            here = at(u, rows)
            mine = pl.ds(pl.multiple_of(place * width, 128), width)
            compute(0, u, x[here, :], x[here, mine])
            hand_on(u).start()

        for hop in range(nz):
            block = u - 1 - hop

            @pl.when(jnp.logical_and(block >= 0, block < blocks))
            def _():
                if hop == 0:
                    hand_on(block).wait_recv()
                    spread.begin(block)
                else:
                    spread.along_z(hop, block)

        ready = u - nz - 1

        @pl.when(ready >= 0)
        def _():
            spread.along_y(ready)
            here = at(ready, rows)
            wide = jnp.concatenate([stream[c, here] for c in range(count)], axis=1)
            compute(1, ready, wide, stream[place, here])
            for i in range(rows // share):
                peer = ready * (rows // share) + i

                @pl.when(peer != place)
                def _():
                    back(peer, place).start()

                @pl.when(peer == place)
                def _():
                    keep_own().start()

        return carry

    lax.fori_loop(0, blocks + nz + 1, step, 0)
    for block in range(blocks):
        hand_on(block).wait_send()
    spread.sent()
    for peer in others(count, place):
        back(peer, place).wait_send()
        back(place, peer).wait_recv()
    keep_own().wait()


def ticks(doc, x, w, wb, bias, in_gain, out_gain, entry, blocks=4):
    count = lax.axis_size("seq")
    heads = entry.shape[0]
    width = heads * HD
    total, d = x.shape
    dma = pltpu.SemaphoreType.DMA
    vmem = pl.BlockSpec(memory_space=pltpu.VMEM)
    return pl.pallas_call(
        functools.partial(ticks_kernel, blocks),
        out_shape=jax.ShapeDtypeStruct((total // count, d), BF16),
        in_specs=[pl.BlockSpec(memory_space=pltpu.SMEM)] + [vmem] * 7,
        out_specs=pl.BlockSpec(memory_space=pl.ANY),
        scratch_shapes=[
            pltpu.VMEM((count, total, width), BF16),
            pltpu.VMEM((TICKS, total, width), BF16),
            pltpu.VMEM((heads, HD, HD), F32),
            dma((blocks,)),
            dma((blocks,)),
            dma((4, count, blocks)),
            dma((count, blocks)),
            dma((count,)),
            dma((count,)),
            dma(()),
        ],
        compiler_params=pltpu.CompilerParams(
            collective_id=1, has_side_effects=True, vmem_limit_bytes=58 * 2**20
        ),
        name="ticks",
    )(doc, x, w, wb, bias, in_gain, out_gain, entry)


def shards(residual, w_qkv, w_beta, beta_bias, norm_gain, out_gain, state_in, doc_start):
    count = lax.axis_size("seq")
    place = lax.axis_index("seq")
    heads = HEADS // count
    stream, weights, betas = start_exchange(residual[0], w_qkv[0], w_beta[0].T)
    stream = stream.reshape(-1, stream.shape[2])
    state = lax.dynamic_slice(state_in[0], (place * heads, 0, 0), (heads, HD, HD))
    out = ticks(
        doc_start[:, 0], stream, weights, betas, beta_bias, norm_gain, out_gain, state
    )
    return out[None]


def solution(mesh):
    return jax.shard_map(
        shards,
        mesh=mesh,
        in_specs=(
            P("section", "seq", None),
            P("section", "seq", None),
            P("section", "seq", None),
            P("section", None),
            P("section", None),
            P("section", None),
            P("section", None, None, None),
            P(None, "section"),
        ),
        out_specs=P("section", "seq", None),
        check_vma=False,
    )
```

```python
import functools

import jax
import jax.numpy as jnp
from jax import lax
from jax.experimental import pallas as pl
from jax.experimental.pallas import tpu as pltpu
from jax.sharding import PartitionSpec as P

HEADS = 16
HD = 128
GROUP = 64
TICKS = 2
CHUNK = 128
F32 = jnp.float32
BF16 = jnp.bfloat16


def mm(a, b):
    return jnp.dot(a.astype(BF16), b.astype(BF16), preferred_element_type=F32)


def mm_nt(a, b):
    return lax.dot_general(
        a.astype(BF16), b.astype(BF16), (((1,), (1,)), ((), ())), preferred_element_type=F32
    )


def unit_norm(p):
    return p * lax.rsqrt(jnp.sum(p * p, axis=-1, keepdims=True) + 1e-06)


def layer_rows(
    normed, w, wb, bias, out_gain, residual, state, heads, first_head, doc_block, first_block
):
    rows = normed.shape[0]
    width = heads * HD
    projected = jnp.dot(normed, w, preferred_element_type=F32)
    logits = mm_nt(normed, wb) + bias
    row = lax.broadcasted_iota(jnp.int32, (CHUNK, CHUNK), 0)
    col = lax.broadcasted_iota(jnp.int32, (CHUNK, CHUNK), 1)
    row1 = lax.broadcasted_iota(jnp.int32, (CHUNK, 1), 0)
    eye = (row == col).astype(F32)
    problems = []
    for h in range(heads):
        q_all = unit_norm(projected[:, h * HD : (h + 1) * HD]).astype(BF16)
        k_all = unit_norm(projected[:, width + h * HD : width + (h + 1) * HD])
        k_all = k_all.astype(BF16).astype(F32)
        v_all = projected[:, 2 * width + h * HD : 2 * width + (h + 1) * HD]
        mine = lax.broadcasted_iota(jnp.int32, logits.shape, 1) == first_head + h
        beta_all = jax.nn.sigmoid(
            jnp.sum(jnp.where(mine, logits, 0.0), axis=-1, keepdims=True)
        )
        for c in range(rows // CHUNK):
            at = slice(c * CHUNK, (c + 1) * CHUNK)
            problems.append((h, c, q_all[at], k_all[at], v_all[at], beta_all[at]))
    systems, inverses, masks = [], [], []
    for h, c, q, k, v, beta in problems:
        start = (doc_block - first_block) * GROUP - c * CHUNK
        inside = jnp.logical_and(start >= 0, start < CHUNK)
        cut = jnp.where(inside, start, 0)
        late_row = row >= cut
        late_col = col >= cut
        same = late_row == late_col
        from_entry = jnp.where(inside, (row1 < cut).astype(F32), 1.0)
        to_exit = (row1 >= cut).astype(F32)
        keep = jnp.where(inside, 0.0, 1.0)
        system = jnp.where(jnp.logical_and(row > col, same), mm_nt(k * beta, k), 0.0)
        systems.append(system)
        masks.append((same, from_entry, to_exit, keep))
        inverses.append(eye - jnp.where((row // 2) == (col // 2), system, 0.0))
    size = 2
    while size < CHUNK:
        level = jnp.logical_and(
            (row // (2 * size)) == (col // (2 * size)), (row // size) != (col // size)
        )
        halves = [mm(jnp.where(level, s, 0.0), x) for s, x in zip(systems, inverses)]
        inverses = [x - mm(x, b) for x, b in zip(inverses, halves)]
        size *= 2
    steps = {}
    for (h, c, q, k, v, beta), inverse, (same, from_entry, to_exit, keep) in zip(
        problems, inverses, masks
    ):
        solved = mm(inverse, jnp.concatenate([v * beta, k * (beta * from_entry)], axis=1))
        scores = jnp.where(jnp.logical_and(row >= col, same), mm_nt(q, k), 0.0)
        lhs = jnp.concatenate([scores, jnp.transpose(k * to_exit)], axis=0)
        both = mm(lhs, solved)
        add = both[:, :HD]
        q_in = q.astype(F32) * from_entry
        through = jnp.concatenate([q_in - both[:CHUNK, HD:], -both[CHUNK:, HD:]], axis=0)
        steps[h, c] = (through.astype(BF16), add, keep)
    pieces = []
    for c in range(rows // CHUNK):
        for h in range(heads):
            through, add, keep = steps[h, c]
            now = state[h]
            moved = jnp.dot(through, now.astype(BF16), preferred_element_type=F32) + add
            state[h] = now * keep + moved[CHUNK:]
            pieces.append(moved[:CHUNK])
    columns = []
    for h in range(heads):
        o = jnp.concatenate([pieces[c * heads + h] for c in range(rows // CHUNK)], axis=0)
        columns.append(
            o * lax.rsqrt(jnp.mean(o * o, axis=-1, keepdims=True) + 1e-05) * out_gain
        )
    mixed = jnp.concatenate(columns, axis=1) if heads > 1 else columns[0]
    return (residual.astype(F32) + mixed).astype(BF16)


MESH = pl.DeviceIdType.MESH
Z_CHIPS = 4


def remote(src, dst, send, recv, **to):
    return pltpu.make_async_remote_copy(
        src_ref=src, dst_ref=dst, send_sem=send, recv_sem=recv, device_id=to, device_id_type=MESH
    )


def grid_place():
    count = lax.axis_size("seq")
    nz = min(Z_CHIPS, count)
    ny = count // nz
    place = lax.axis_index("seq")
    return count, nz, ny, place, place // ny, lax.rem(place, ny)


class Spread:
    def __init__(self, slot, blocks, send, recv):
        self.slot, self.blocks, self.send, self.recv = slot, blocks, send, recv
        self.count, self.nz, self.ny, self.place, self.z, self.y = grid_place()
        self.ways = [
            (self.z + 1 < self.nz, self.place + self.ny),
            (self.z > 0, self.place - self.ny),
            (self.y + 1 < self.ny, self.place + 1),
            (self.y > 0, self.place - 1),
        ]

    def neighbours(self):
        return self.ways[: 4 if self.ny > 1 else 2]

    def copy(self, way, source, block, ref=None):
        here = self.slot(source, block)
        return remote(
            here if ref is None else ref,
            here,
            self.send.at[way, source, block],
            self.recv.at[source, block],
            seq=self.ways[way][1],
        )

    def go(self, way, source, block, ref=None):
        if way >= 2 and self.ny == 1:
            return

        @pl.when(self.ways[way][0])
        def _():
            self.copy(way, source, block, ref).start()

    def begin(self, block, ref=None):
        for way in (0, 1, 2, 3):
            self.go(way, self.place, block, ref)

    def arrived(self, source, block):
        self.copy(0, source, block).wait_recv()

    def along_z(self, hop, block):
        for way, sign in ((0, -1), (1, 1)):
            z = self.z + sign * hop

            @pl.when(jnp.logical_and(z >= 0, z < self.nz))
            def _():
                source = z * self.ny + self.y
                self.arrived(source, block)
                if hop + 1 < self.nz:
                    self.go(way, source, block)
                self.go(2, source, block)
                self.go(3, source, block)

    def along_y(self, block):
        for hop in range(1, self.ny):
            for way, sign in ((2, -1), (3, 1)):
                y = self.y + sign * hop

                @pl.when(jnp.logical_and(y >= 0, y < self.ny))
                def _():
                    for z in range(self.nz):
                        self.arrived(z * self.ny + y, block)
                        if hop + 1 < self.ny:
                            self.go(way, z * self.ny + y, block)

    def sent(self):
        def one(i, carry):
            source, block = i // self.blocks, lax.rem(i, self.blocks)
            z, y = source // self.ny, lax.rem(source, self.ny)
            lines = [
                jnp.logical_and(y == self.y, z <= self.z),
                jnp.logical_and(y == self.y, z >= self.z),
                y <= self.y,
                y >= self.y,
            ]
            for way in range(4 if self.ny > 1 else 2):

                @pl.when(jnp.logical_and(lines[way], self.ways[way][0]))
                def _():
                    self.copy(way, source, block).wait_send()

            return carry

        lax.fori_loop(0, self.count * self.blocks, one, 0)


def others(count, place):
    return [lax.rem(place + hop, count) for hop in range(1, count)]


def greet_all(count, place):
    barrier = pltpu.get_barrier_semaphore()
    for peer in others(count, place):
        pl.semaphore_signal(barrier, inc=1, device_id={"seq": peer}, device_id_type=MESH)
    pl.semaphore_wait(barrier, count - 1)


def start_kernel(
    blocks, x, w, wb, stream, weights, betas, send, recv, w_send, w_recv, b_send, b_recv, own
):
    count, nz, ny, place, _, _ = grid_place()
    depth = w.shape[0]
    width = weights.shape[1] // 3
    greet_all(count, place)
    rows = x.shape[0] // blocks

    def piece(block):
        return pl.ds(pl.multiple_of(block * rows, 16), rows)

    spread = Spread(lambda source, block: stream.at[source, piece(block)], blocks, send, recv)
    for block in range(blocks):
        spread.begin(block, x.at[piece(block)])

    def columns(peer, part):
        at = pl.multiple_of((part * count + peer) * width, 128)
        return w.at[:, pl.ds(at, width)]

    def landing(source, part):
        return weights.at[
            pl.ds(pl.multiple_of(source * depth, 16), depth), part * width : (part + 1) * width
        ]

    def beta_copy(hop, peer, source):
        return remote(wb, betas.at[source], b_send.at[hop], b_recv.at[hop], seq=peer)

    def weight_copy(hop, peer, source, part):
        return remote(
            columns(peer, part), landing(source, part), w_send.at[hop, part],
            w_recv.at[hop, part], seq=peer,
        )

    for hop, peer in enumerate(others(count, place)):
        beta_copy(hop, peer, place).start()
        for part in range(3):
            weight_copy(hop, peer, place, part).start()
    local = [
        pltpu.make_async_copy(x, stream.at[place], own.at[0]),
        pltpu.make_async_copy(wb, betas.at[place], own.at[1]),
    ] + [
        pltpu.make_async_copy(columns(place, part), landing(place, part), own.at[2 + part])
        for part in range(3)
    ]
    for one in local:
        one.start()
    for hop in range(1, nz):
        for block in range(blocks):
            spread.along_z(hop, block)
    for block in range(blocks):
        spread.along_y(block)
    for hop, peer in enumerate(others(count, place)):
        source = lax.rem(place + count - hop - 1, count)
        beta_copy(hop, peer, source).wait_recv()
        beta_copy(hop, peer, place).wait_send()
        for part in range(3):
            weight_copy(hop, peer, source, part).wait_recv()
            weight_copy(hop, peer, place, part).wait_send()
    spread.sent()
    for one in local:
        one.wait()


def start_exchange(x, w, wb, blocks=4):
    count = lax.axis_size("seq")
    any_space = pl.BlockSpec(memory_space=pl.ANY)
    dma = pltpu.SemaphoreType.DMA
    return pl.pallas_call(
        functools.partial(start_kernel, blocks),
        out_shape=(
            jax.ShapeDtypeStruct((count,) + x.shape, x.dtype),
            jax.ShapeDtypeStruct((count * w.shape[0], w.shape[1] // count), w.dtype),
            jax.ShapeDtypeStruct((count,) + wb.shape, wb.dtype),
        ),
        in_specs=[any_space] * 3,
        out_specs=(any_space,) * 3,
        scratch_shapes=[
            dma((4, count, blocks)),
            dma((count, blocks)),
            dma((count - 1, 3)),
            dma((count - 1, 3)),
            dma((count - 1,)),
            dma((count - 1,)),
            dma((5,)),
        ],
        compiler_params=pltpu.CompilerParams(collective_id=0, has_side_effects=True),
        name="start_exchange",
    )(x, w, wb)


def ticks_kernel(
    blocks, doc, x, w, wb, bias, in_gain, out_gain, entry, result,
    stream, outs, state, x_send, x_recv, send, recv, back_send, back_recv, own,
):
    count, nz, ny, place, _, _ = grid_place()
    sections = lax.axis_size("section")
    section = lax.axis_index("section")
    after, before = lax.rem(section + 1, sections), lax.rem(section + sections - 1, sections)
    heads = HEADS // count
    width = heads * HD
    rows = x.shape[0] // blocks
    share = x.shape[0] // count

    def at(block, size):
        return pl.ds(pl.multiple_of(block * size, 16), size)

    def slot(source, block):
        return stream.at[source, at(block, rows)]

    spread = Spread(slot, blocks, send, recv)
    barrier = pltpu.get_barrier_semaphore()
    for peer in others(count, place):
        pl.semaphore_signal(barrier, inc=1, device_id={"seq": peer}, device_id_type=MESH)
    for peer in (after, before):
        pl.semaphore_signal(barrier, inc=1, device_id={"section": peer}, device_id_type=MESH)
    pl.semaphore_wait(barrier, count + 1)

    def hand_on(block):
        return remote(
            outs.at[0, at(block, rows)], slot(place, block),
            x_send.at[block], x_recv.at[block], section=after,
        )

    def columns(source):
        return result.at[:, pl.ds(pl.multiple_of(source * width, 128), width)]

    def back(peer, source):
        return remote(
            outs.at[1, at(peer, share)], columns(source),
            back_send.at[peer], back_recv.at[source], seq=peer,
        )

    def keep_own():
        return pltpu.make_async_copy(outs.at[1, at(place, share)], columns(place), own)

    def compute(tick, block, wide, residual):
        wide = wide.astype(F32)
        scale = lax.rsqrt(jnp.mean(wide * wide, axis=-1, keepdims=True) + 1e-05)
        normed = (wide * scale * in_gain[...]).astype(BF16)
        now = [state[h] for h in range(heads)]
        outs[tick, at(block, rows)] = layer_rows(
            normed, w[...], jnp.concatenate([wb[c] for c in range(count)], axis=1), bias[...],
            out_gain[...], residual, now, heads, place * heads, doc[tick], block * (rows // GROUP),
        )
        for h in range(heads):
            state[h] = now[h]

    state[...] = entry[...]

    def step(u, carry):
        @pl.when(u < blocks)
        def _():
            here = at(u, rows)
            mine = pl.ds(pl.multiple_of(place * width, 128), width)
            compute(0, u, x[here, :], x[here, mine])
            hand_on(u).start()

        for hop in range(nz):
            block = u - 1 - hop

            @pl.when(jnp.logical_and(block >= 0, block < blocks))
            def _():
                if hop == 0:
                    hand_on(block).wait_recv()
                    spread.begin(block)
                else:
                    spread.along_z(hop, block)

        ready = u - nz - 1

        @pl.when(ready >= 0)
        def _():
            spread.along_y(ready)
            here = at(ready, rows)
            wide = jnp.concatenate([stream[c, here] for c in range(count)], axis=1)
            compute(1, ready, wide, stream[place, here])
            for i in range(rows // share):
                peer = ready * (rows // share) + i

                @pl.when(peer != place)
                def _():
                    back(peer, place).start()

                @pl.when(peer == place)
                def _():
                    keep_own().start()

        return carry

    lax.fori_loop(0, blocks + nz + 1, step, 0)
    for block in range(blocks):
        hand_on(block).wait_send()
    spread.sent()
    for peer in others(count, place):
        back(peer, place).wait_send()
        back(place, peer).wait_recv()
    keep_own().wait()


def ticks(doc, x, w, wb, bias, in_gain, out_gain, entry, blocks=4):
    count = lax.axis_size("seq")
    heads = entry.shape[0]
    width = heads * HD
    total, d = x.shape
    dma = pltpu.SemaphoreType.DMA
    vmem = pl.BlockSpec(memory_space=pltpu.VMEM)
    return pl.pallas_call(
        functools.partial(ticks_kernel, blocks),
        out_shape=jax.ShapeDtypeStruct((total // count, d), BF16),
        in_specs=[pl.BlockSpec(memory_space=pltpu.SMEM)] + [vmem] * 7,
        out_specs=pl.BlockSpec(memory_space=pl.ANY),
        scratch_shapes=[
            pltpu.VMEM((count, total, width), BF16),
            pltpu.VMEM((TICKS, total, width), BF16),
            pltpu.VMEM((heads, HD, HD), F32),
            dma((blocks,)),
            dma((blocks,)),
            dma((4, count, blocks)),
            dma((count, blocks)),
            dma((count,)),
            dma((count,)),
            dma(()),
        ],
        compiler_params=pltpu.CompilerParams(
            collective_id=1, has_side_effects=True, vmem_limit_bytes=58 * 2**20
        ),
        name="ticks",
    )(doc, x, w, wb, bias, in_gain, out_gain, entry)


def shards(residual, w_qkv, w_beta, beta_bias, norm_gain, out_gain, state_in, doc_start):
    count = lax.axis_size("seq")
    place = lax.axis_index("seq")
    heads = HEADS // count
    stream, weights, betas = start_exchange(residual[0], w_qkv[0], w_beta[0].T)
    stream = stream.reshape(-1, stream.shape[2])
    state = lax.dynamic_slice(state_in[0], (place * heads, 0, 0), (heads, HD, HD))
    out = ticks(
        doc_start[:, 0], stream, weights, betas, beta_bias, norm_gain, out_gain, state
    )
    return out[None]


def solution(mesh):
    return jax.shard_map(
        shards,
        mesh=mesh,
        in_specs=(
            P("section", "seq", None),
            P("section", "seq", None),
            P("section", "seq", None),
            P("section", None),
            P("section", None),
            P("section", None),
            P("section", None, None, None),
            P(None, "section"),
        ),
        out_specs=P("section", "seq", None),
        check_vma=False,
    )
```
